256 devices in a mesh: seq: 32 (over y, z), head: 8 (over x, core).
Axes of the slice: x: 4, y: 4, z: 8, core: 2. Of those that a mesh axis runs over, the one named last changes fastest.
Arguments:
- queries: bfloat16 [24576, 4096], P('seq', 'head'), may hold values from -120 to 120
- residual: bfloat16 [24576, 8192], P('seq', 'head'), may hold values from -3 to 3
- nbr_kv: bfloat16 [512, 2, 128, 4096], P('seq', None, None, 'head'), may hold values from -12 to 12
- nbr_owner: int32 [384, 2], P('seq'), may hold values from 0 to 31, all different within a row; in each aligned block of 12 rows (0 to 11, 12 to 23, ...) at most 2 rows name the same one
- nbr_slot: int32 [384, 2], P('seq'), may hold values from 0 to 15
- out_weight: bfloat16 [4096, 8192], P('seq', 'head'), may hold values from -0.09375 to 0.09375
Outputs:
- mixed: bfloat16 [24576, 8192], P('seq', 'head')
The draws below stay inside these ranges and needn't reach their ends.
Inputs may be any that keep to these rules, and one draw needn't show every extreme that they name: `nbr_owner`: the two owners of a block differ. Among the 12 blocks of one index of seq no owner is named more than 2 times, and this is reached.
All inputs are finite; a program needn't handle non-finite values.
Results may differ from the reference program's by a relative error of at most 0.008.
Values may be sent and summed in bfloat16 or wider, within the bound.
No kernel may reach another device: no remote copies, remote signals or barrier semaphores. Data moves between devices by JAX's collectives and lax.ppermute only.
A program may use at most 128 MiB of HBM per device.

```python
import math
import jax
import jax.numpy as jnp
import numpy as np
from jax import lax

D = 8192
HEADS = 32
HDIM = 128
BLOCK = 64
NBR_LEN = 128
NEIGHBOURS = 2
SLOTS_DEV = 16
HD = 4096
BLOCKS_DEV = 12
TOKENS = 24576
BLOCKS = 384
SLOTS = 512
MOST = 2
N_SEQ = 32


def draw_queries(key, part):
    key = jax.random.fold_in(key, 1)
    values = jax.random.normal(key, (TOKENS, HD), jnp.float32)
    return jnp.clip(values, -120.0, 120.0).astype(jnp.bfloat16)


def draw_nbr_kv(key, part):
    key = jax.random.fold_in(key, 2)
    draw_one = jax.random.fold_in(key, 0)
    scale_pair = jnp.array([1.0, 2.0], jnp.float32)[None, :, None, None]
    stacked = jax.random.normal(draw_one, (SLOTS, 2, NBR_LEN, HD), jnp.float32) * scale_pair
    return jnp.clip(stacked, -12.0, 12.0).astype(jnp.bfloat16)


def touch_ends(drawn, own_key, low, top_value):
    longest = drawn.shape.index(max(drawn.shape))
    spots = []
    for shift in (0, 1):
        where = [jax.random.randint(jax.random.fold_in(own_key, axis), (), 0, length) for axis, length in enumerate(drawn.shape)]
        where[longest] = (where[longest] + shift) % drawn.shape[longest]
        spots.append(tuple(where))
    return drawn.at[spots[0]].set(low).at[spots[1]].set(top_value)


def shard_levels(key, dims, pieces, least, high):
    factor_of, own = 1.0, jax.random.fold_in(key, 6)
    for dim, blocks in pieces:
        steps = jnp.exp(jax.random.uniform(jax.random.fold_in(own, dim), (blocks,), jnp.float32, least / len(pieces), high / len(pieces)))
        factor_of = factor_of * jnp.repeat(steps, dims[dim] // blocks).reshape([-1 if axis == dim else 1 for axis in range(len(dims))])
    return factor_of


def shared_out(stream_key, own, number, rows, count, top, limit, lean):
    ranking = jax.random.permutation(stream_key, count)
    crowded, ordinary = shares(count, rows * top, limit, lean, True), shares(count, rows * top, limit, lean, False)
    places = jnp.arange(count)

    def named(lengths, offset_by):
        used = int((lengths > 0).sum())
        fixed = max(1, used // 4)
        moved = fixed + (places - fixed + offset_by * (used - fixed)) % max(1, count - fixed)
        return jnp.zeros((count,), jnp.int32).at[ranking[jnp.where(places < fixed, places, moved)]].set(jnp.asarray(lengths, jnp.int32))

    lengths = jnp.where(number % 4 == 0, named(crowded, number // 4), named(ordinary, number - number // 4 - 1))
    mixed = jax.random.permutation(jax.random.fold_in(own, 3), count)
    giver, receiver = mixed[0:count // 2 * 2:2], mixed[1:count // 2 * 2:2]
    margin = jnp.minimum(lengths[giver] - 1, limit - lengths[receiver]) // 2
    margin = jnp.where((giver == ranking[0]) | (receiver == ranking[0]) | (lengths[receiver] == 0), 0, jnp.maximum(margin, 0))
    moved = jax.random.randint(jax.random.fold_in(own, 4), (count // 2,), 0, 1 << 20) % (margin + 1)
    lengths = lengths.at[giver].add(-moved).at[receiver].add(moved)
    labels = jnp.searchsorted(jnp.cumsum(lengths), jnp.arange(rows * top), side="right").astype(jnp.int32)
    listing = labels.reshape(top, rows).T
    listing = listing[jax.random.permutation(jax.random.fold_in(own, 1), rows)]
    offset_by = jax.random.randint(jax.random.fold_in(own, 2), (rows, 1), 0, top)
    return jnp.take_along_axis(listing, (jnp.arange(top)[None, :] + offset_by) % top, axis=1)


def shares(count, total, limit, skew, full):
    weights = [(1 << 20) // math.isqrt(standing ** skew) + 1 for standing in range(1, count + 1)]
    largest = limit if full else min(limit, max(-(-total // count), total * weights[0] // sum(weights)))
    least = 1 if total - largest >= count - 1 else 0
    counts, rest = [largest] + [least] * (count - 1), total - largest - least * (count - 1)
    while rest > 0:
        candidates = [i for i in range(1, count) if counts[i] < largest] or [i for i in range(1, count) if counts[i] < limit]
        mass, budget = sum([weights[i] for i in candidates]), rest
        for i in candidates:
            addition = min(limit - counts[i], max(1, budget * weights[i] // mass), rest)
            counts[i] = counts[i] + addition
            rest = rest - addition
    return np.array(counts)


def bell_draw(own_key, shape, scale, limit, cuts=(), held_as=jnp.bfloat16):
    entries = scale * jax.random.normal(own_key, shape, jnp.float32)
    if cuts:
        entries = entries * shard_levels(own_key, shape, cuts, -0.22, 0.18)
    return jnp.clip(entries, -limit, limit).astype(held_as)


def setup_inputs(seed: int = 0) -> dict:
    key_list = jax.random.split(jax.random.key(seed), 7)
    queries = draw_queries(jax.random.fold_in(key_list[6], 71), 0)
    residual = bell_draw(key_list[1], (TOKENS, D), 0.5, 3.0, ((0, 32), (1, 8)))
    nbr_kv = draw_nbr_kv(jax.random.fold_in(key_list[6], 71), 0)
    nbr_owner_keys = jax.random.split(jax.random.fold_in(key_list[3], 1), BLOCKS // BLOCKS_DEV)
    nbr_owner_turns = jax.random.permutation(jax.random.fold_in(key_list[3], 3), BLOCKS // BLOCKS_DEV)
    nbr_owner = jax.vmap(lambda own, number: shared_out(jax.random.fold_in(key_list[3], 2), own, number, BLOCKS_DEV, N_SEQ, NEIGHBOURS, MOST, 2))(nbr_owner_keys, nbr_owner_turns).reshape((BLOCKS, NEIGHBOURS))
    nbr_slot = touch_ends(jax.random.randint(key_list[4], (BLOCKS, NEIGHBOURS), 0, SLOTS_DEV), jax.random.fold_in(key_list[4], 1), 0, SLOTS_DEV - 1).astype(jnp.int32)
    out_weight = bell_draw(key_list[5], (HD, D), HD ** -0.5, 0.09375, ((0, 32), (1, 8)))
    return {"queries": queries, "residual": residual, "nbr_kv": nbr_kv, "nbr_owner": nbr_owner, "nbr_slot": nbr_slot, "out_weight": out_weight}


def reference(queries, residual, nbr_kv, nbr_owner, nbr_slot, out_weight):
    total_rows = queries.shape[0]
    feat_width = queries.shape[1]
    shift_rows = BLOCK - 1
    group_count = total_rows // BLOCK
    shifted = jnp.concatenate([queries[shift_rows:], jnp.zeros((shift_rows, feat_width), jnp.bfloat16)], axis=0)
    shifted = shifted.reshape(group_count, BLOCK, HEADS, HDIM)
    slot_rows = (nbr_owner * SLOTS_DEV + nbr_slot).astype(jnp.int32)

    def one_group(pair_args):
        query_block, slot_pair = pair_args
        chosen = jnp.take(nbr_kv, slot_pair, axis=0)
        key_rows = chosen[:, 0].reshape(NEIGHBOURS, NBR_LEN, HEADS, HDIM).astype(jnp.float32)
        values = chosen[:, 1].reshape(NEIGHBOURS, NBR_LEN, HEADS, HDIM).astype(jnp.float32)
        scores = jnp.einsum("qhd,jkhd->hqjk", query_block.astype(jnp.float32), key_rows) * HDIM ** -0.5
        row_max = jnp.max(scores, axis=-1)
        weights = jnp.exp(scores - row_max[..., None])
        weight_sum = jnp.sum(weights, axis=-1)
        rounded = lax.optimization_barrier(weights.astype(jnp.bfloat16)).astype(jnp.float32)
        blended = jnp.einsum("hqjk,jkhd->jqhd", rounded, values)
        partial_value = (blended / jnp.transpose(weight_sum, (2, 1, 0))[..., None]).astype(jnp.bfloat16)
        partial_value = lax.optimization_barrier(partial_value).astype(jnp.float32)
        joint = jnp.max(row_max, axis=-1, keepdims=True)
        factor = jnp.exp(row_max - joint) * weight_sum
        factor = jnp.transpose(factor, (2, 1, 0))[..., None]
        result = jnp.sum(factor * partial_value, axis=0) / jnp.sum(factor, axis=0)
        return result.astype(jnp.bfloat16).reshape(BLOCK, HEADS * HDIM)

    attended = lax.map(one_group, (shifted, slot_rows)).reshape(total_rows, feat_width)
    placed = jnp.concatenate([jnp.zeros((shift_rows, feat_width), jnp.bfloat16), attended[:total_rows - shift_rows]], axis=0)
    projected = jnp.dot(placed, out_weight, preferred_element_type=jnp.float32)
    return (residual.astype(jnp.float32) + projected).astype(jnp.bfloat16)
```

```python
import jax
import jax.numpy as jnp
from jax import lax
from jax.experimental import pallas as pl
from jax.experimental.pallas import tpu as pltpu
from jax.sharding import PartitionSpec as P

HDIM = 128
BLOCK = 64
KEPT = BLOCK - 1
STAT_ROWS = 8
NAMED = 2
VMEM = pl.BlockSpec(memory_space=pltpu.VMEM)


def call(kernel, name, scalars, inputs, outputs, limit, flops=0, moved=0):
    return pl.pallas_call(
        kernel,
        grid_spec=pltpu.PrefetchScalarGridSpec(
            num_scalar_prefetch=len(scalars),
            grid=(),
            in_specs=[VMEM] * len(inputs),
            out_specs=[VMEM] * len(outputs),
        ),
        out_shape=outputs,
        compiler_params=pltpu.CompilerParams(vmem_limit_bytes=limit << 20),
        cost_estimate=pl.CostEstimate(flops=flops, bytes_accessed=moved, transcendentals=0),
        name=name,
    )(*scalars, *inputs)


def like(shape):
    return jax.ShapeDtypeStruct(shape, jnp.bfloat16)


def spread(value):
    high = value.astype(jnp.bfloat16).astype(jnp.float32)
    rest = value - high
    middle = rest.astype(jnp.bfloat16).astype(jnp.float32)
    return jnp.concatenate([high, middle, rest - middle], axis=1)


def send_kernel(target, query_ref, next_ref, out_ref):
    blocks, rows, width = query_ref.shape
    kept = lax.broadcasted_iota(jnp.int32, (rows, width), 0) < rows - 1
    for block in range(blocks):
        after = query_ref[block + 1] if block + 1 < blocks else next_ref[...]
        turned = jnp.where(kept, after, query_ref[block])
        for index in range(2):
            out_ref[target[2 * block + index]] = turned


def attend_kernel(order, slots, count, query_ref, kv_ref, out_ref):
    width = query_ref.shape[2]
    heads = width // HDIM
    lane = lax.broadcasted_iota(jnp.int32, (BLOCK, HDIM), 1)

    def one(index, carry):
        place = order[index]
        slot = slots[place]
        stats = jnp.zeros((BLOCK, HDIM), jnp.float32)
        for head in range(heads):
            cols = slice(head * HDIM, (head + 1) * HDIM)
            scores = lax.dot_general(
                query_ref[place, :, cols],
                kv_ref[slot, 0, :, cols],
                (((1,), (1,)), ((), ())),
                preferred_element_type=jnp.float32,
            ) * HDIM ** (-0.5)
            top = jnp.max(scores, axis=1, keepdims=True)
            weights = jnp.exp(scores - top)
            total = jnp.sum(weights, axis=1, keepdims=True)
            blended = jnp.dot(
                weights.astype(jnp.bfloat16),
                kv_ref[slot, 1, :, cols],
                preferred_element_type=jnp.float32,
            )
            out_ref[place, :BLOCK, cols] = (blended / total).astype(jnp.bfloat16)
            stats = jnp.where(lane == head, top, stats)
            stats = jnp.where(lane == heads + head, total, stats)
        pieces = spread(stats.T[:STAT_ROWS])
        filler = jnp.zeros((STAT_ROWS, width - 3 * BLOCK), jnp.float32)
        out_ref[place, BLOCK:, :] = jnp.concatenate([pieces, filler], axis=1).astype(jnp.bfloat16)
        return carry

    lax.fori_loop(0, count[0], one, 0)


def combine_kernel(target, parts_ref, out_ref, last_ref):
    blocks, rows, width = out_ref.shape
    heads = width // HDIM
    kept = lax.broadcasted_iota(jnp.int32, (rows, width), 0) < rows - 1

    def joined(block):
        tops, sums = [], []
        places = [target[2 * block + index] for index in range(2)]
        for place in places:
            pieces = parts_ref[place, rows:, :].astype(jnp.float32)
            stats = pieces[:, :rows] + pieces[:, rows : 2 * rows] + pieces[:, 2 * rows : 3 * rows]
            tops.append(stats[:heads])
            sums.append(stats[heads : 2 * heads])
        joint = jnp.maximum(tops[0], tops[1])
        factors = [jnp.exp(top - joint) * total for top, total in zip(tops, sums)]
        whole = factors[0] + factors[1]
        shares = jnp.concatenate([factors[0] / whole, factors[1] / whole], axis=0)
        shares = jnp.concatenate([shares] * (HDIM // (2 * heads)), axis=0)
        columns = jnp.concatenate([shares, shares], axis=1).T[:rows]
        merged = []
        for head in range(heads):
            cols = slice(head * HDIM, (head + 1) * HDIM)
            first, second = (parts_ref[place, :rows, cols].astype(jnp.float32) for place in places)
            merged.append(columns[:, head : head + 1] * first + columns[:, heads + head : heads + head + 1] * second)
        return jnp.concatenate(merged, axis=1)

    before = joined(0)
    out_ref[0] = before.astype(jnp.bfloat16)
    for block in range(1, blocks):
        now = joined(block)
        out_ref[block] = jnp.where(kept, before, now).astype(jnp.bfloat16)
        before = now
    last_ref[...] = before.astype(jnp.bfloat16)


def swap(value):
    return lax.all_to_all(value, "seq", split_axis=0, concat_axis=0, tiled=True)


def shards(queries, residual, nbr_kv, nbr_owner, nbr_slot, out_weight):
    tok_rows, width = queries.shape
    blocks = tok_rows // BLOCK
    seq_count = lax.axis_size("seq")
    places = seq_count * NAMED
    all_weight = lax.all_gather(out_weight, "seq", axis=0, tiled=True)

    owners = nbr_owner.reshape(-1)
    position = jnp.arange(owners.shape[0], dtype=jnp.int32)
    earlier = (owners[:, None] == owners[None, :]) & (position[None, :] < position[:, None])
    target = owners * NAMED + jnp.sum(earlier.astype(jnp.int32), axis=1)
    place = jnp.arange(places, dtype=jnp.int32)
    match = (place[:, None] == target[None, :]).astype(jnp.int32)
    asked = jnp.sum(match * (nbr_slot.reshape(-1) + 1)[None, :], axis=1)
    heard = swap(asked.reshape(seq_count, NAMED)).reshape(-1)

    first_next = lax.ppermute(queries[:BLOCK], "seq", [(s, s - 1) for s in range(1, seq_count)])
    chunks = queries.reshape(blocks, BLOCK, width)
    (sent,) = call(send_kernel, "send", [target], [chunks, first_next], [like((places, BLOCK, width))], 16)
    arrived = swap(sent)

    takes = (heard > 0).astype(jnp.int32)
    rank = jnp.cumsum(takes) - takes
    order = jnp.sum(jnp.where((takes[None, :] > 0) & (rank[None, :] == place[:, None]), place[None, :], 0), axis=1)
    (partial,) = call(
        attend_kernel,
        "attend",
        [order, jnp.maximum(heard - 1, 0), jnp.sum(takes).reshape(1)],
        [arrived, nbr_kv],
        [like((places, BLOCK + STAT_ROWS, width))],
        32,
    )
    moved, last = call(
        combine_kernel, "combine", [target], [swap(partial)], [like((blocks, BLOCK, width)), like((BLOCK, width))], 32
    )
    carried = lax.ppermute(last, "seq", [(s, s + 1) for s in range(seq_count - 1)])
    chunk = lax.broadcasted_iota(jnp.int32, (blocks, 1, 1), 0)
    row = lax.broadcasted_iota(jnp.int32, (1, BLOCK, 1), 1)
    placed = jnp.where((chunk == 0) & (row < KEPT), carried[None], moved).reshape(tok_rows, width)
    every_head = lax.all_gather(placed, "head", axis=1, tiled=True)
    projected = jnp.dot(every_head, all_weight, preferred_element_type=jnp.float32)
    return (residual.astype(jnp.float32) + projected).astype(jnp.bfloat16)


def solution(mesh):
    return jax.shard_map(
        shards,
        mesh=mesh,
        in_specs=(
            P("seq", "head"),
            P("seq", "head"),
            P("seq", None, None, "head"),
            P("seq", None),
            P("seq", None),
            P("seq", "head"),
        ),
        out_specs=P("seq", "head"),
        check_vma=False,
    )
```

```python
import jax
import jax.numpy as jnp
from jax import lax
from jax.experimental import pallas as pl
from jax.experimental.pallas import tpu as pltpu
from jax.sharding import PartitionSpec as P

HDIM = 128
BLOCK = 64
KEPT = BLOCK - 1
STAT_ROWS = 8
NAMED = 2
AT_ONCE = 2
VMEM = pl.BlockSpec(memory_space=pltpu.VMEM)


def call(kernel, name, scalars, inputs, outputs, limit, scratch=()):
    return pl.pallas_call(
        kernel,
        grid_spec=pltpu.PrefetchScalarGridSpec(
            num_scalar_prefetch=len(scalars),
            grid=(),
            in_specs=[VMEM] * len(inputs),
            out_specs=[VMEM] * len(outputs),
            scratch_shapes=scratch,
        ),
        out_shape=outputs,
        compiler_params=pltpu.CompilerParams(vmem_limit_bytes=limit << 20),
        name=name,
    )(*scalars, *inputs)


def like(shape):
    return jax.ShapeDtypeStruct(shape, jnp.bfloat16)


def spread(value):
    high = value.astype(jnp.bfloat16).astype(jnp.float32)
    rest = value - high
    middle = rest.astype(jnp.bfloat16).astype(jnp.float32)
    return jnp.concatenate([high, middle, rest - middle], axis=1)


def send_kernel(target, info, query_ref, next_ref, out_ref):
    blocks, rows, width = query_ref.shape
    kept = lax.broadcasted_iota(jnp.int32, (rows, width), 0) < rows - 1
    lane = lax.broadcasted_iota(jnp.int32, (STAT_ROWS, width), 1)
    for owner in range(out_ref.shape[0]):
        ids = jnp.where(lane == 0, info[NAMED * owner], 0) + jnp.where(lane == 1, info[NAMED * owner + 1], 0)
        out_ref[owner, NAMED * rows :, :] = ids.astype(jnp.float32).astype(jnp.bfloat16)
    for block in range(blocks):
        after = query_ref[block + 1] if block + 1 < blocks else next_ref[...]
        turned = jnp.where(kept, after, query_ref[block])
        for index in range(2):
            place = target[2 * block + index]
            start = pl.multiple_of(lax.rem(place, NAMED) * rows, rows)
            out_ref[lax.div(place, NAMED), pl.ds(start, rows), :] = turned


def attend_kernel(heard, query_ref, kv_ref, out_ref, listed):
    places = heard.shape[0]
    width = query_ref.shape[2]
    pair = 2 * HDIM
    zero = jnp.zeros((BLOCK, HDIM), jnp.bfloat16)

    def note(place, count):
        @pl.when(heard[place] > 0)
        def _():
            listed[count] = place

        return count + (heard[place] > 0).astype(jnp.int32)

    count = lax.fori_loop(0, places, note, 0)

    def some(index, carry):
        work = []
        for other in range(AT_ONCE):
            place = listed[jnp.minimum(index * AT_ONCE + other, count - 1)]
            slot = heard[place] - 1
            start = pl.multiple_of(lax.rem(place, NAMED) * BLOCK, BLOCK)
            for first in range(0, width, pair):
                work.append((place, slot, lax.div(place, NAMED), start, first))
        scores = []
        for place, slot, source, start, first in work:
            left = query_ref[source, pl.ds(start, BLOCK), first : first + HDIM]
            right = query_ref[source, pl.ds(start, BLOCK), first + HDIM : first + pair]
            both = jnp.concatenate(
                [jnp.concatenate([left, zero], axis=1), jnp.concatenate([zero, right], axis=1)], axis=0
            )
            scores.append(
                lax.dot_general(
                    kv_ref[slot, 0, :, first : first + pair],
                    both,
                    (((1,), (1,)), ((), ())),
                    preferred_element_type=jnp.float32,
                )
                * HDIM ** (-0.5)
            )
        tops = [jnp.max(score, axis=0, keepdims=True) for score in scores]
        weights = [jnp.exp(score - top) for score, top in zip(scores, tops)]
        totals = [jnp.sum(weight, axis=0, keepdims=True) for weight in weights]
        shares = [(weight * (1.0 / total)).astype(jnp.bfloat16) for weight, total in zip(weights, totals)]
        for (place, slot, source, start, first), share in zip(work, shares):
            blended = lax.dot_general(
                share,
                kv_ref[slot, 1, :, first : first + pair],
                (((0,), (0,)), ((), ())),
                preferred_element_type=jnp.float32,
            )
            out_ref[place, :BLOCK, first : first + HDIM] = blended[:BLOCK, :HDIM].astype(jnp.bfloat16)
            out_ref[place, :BLOCK, first + HDIM : first + pair] = blended[BLOCK:, HDIM:].astype(jnp.bfloat16)
        pairs = width // pair
        for other in range(AT_ONCE):
            own = slice(other * pairs, (other + 1) * pairs)
            rows = jnp.concatenate(
                tops[own] + totals[own] + [jnp.zeros((STAT_ROWS - 2 * pairs, HDIM), jnp.float32)], axis=0
            )
            pieces = [spread(rows), jnp.zeros((STAT_ROWS, width - 3 * HDIM), jnp.float32)]
            out_ref[work[other * pairs][0], BLOCK:, :] = jnp.concatenate(pieces, axis=1).astype(jnp.bfloat16)
        return carry

    lax.fori_loop(0, lax.div(count + AT_ONCE - 1, AT_ONCE), some, 0)


def combine_kernel(target, parts_ref, out_ref, last_ref):
    blocks, rows, width = out_ref.shape
    pairs = width // (2 * HDIM)
    kept = lax.broadcasted_iota(jnp.int32, (rows, width), 0) < rows - 1

    def joined(block):
        tops, sums = [], []
        places = [target[2 * block + index] for index in range(2)]
        for place in places:
            pieces = parts_ref[place, rows:, :].astype(jnp.float32)
            stats = pieces[:, :HDIM] + pieces[:, HDIM : 2 * HDIM] + pieces[:, 2 * HDIM : 3 * HDIM]
            tops.append(stats[:pairs])
            sums.append(stats[pairs : 2 * pairs])
        joint = jnp.maximum(tops[0], tops[1])
        factors = [jnp.exp(top - joint) * total for top, total in zip(tops, sums)]
        whole = factors[0] + factors[1]
        shares = jnp.concatenate([factors[0] / whole, factors[1] / whole], axis=0)
        columns = jnp.concatenate([shares] * (HDIM // (2 * pairs)), axis=0).T
        merged = []
        for head in range(2 * pairs):
            cols = slice(head * HDIM, (head + 1) * HDIM)
            own = slice(head % 2 * rows, head % 2 * rows + rows)
            first, second = (parts_ref[place, :rows, cols].astype(jnp.float32) for place in places)
            at = head // 2
            merged.append(columns[own, at : at + 1] * first + columns[own, pairs + at : pairs + at + 1] * second)
        return jnp.concatenate(merged, axis=1)

    before = joined(0)
    out_ref[0] = before.astype(jnp.bfloat16)
    for block in range(1, blocks):
        now = joined(block)
        out_ref[block] = jnp.where(kept, before, now).astype(jnp.bfloat16)
        before = now
    last_ref[...] = before.astype(jnp.bfloat16)


def early_kernel(_, *refs):
    *refs, out_ref = refs
    count = len(refs) // 2
    total = None
    for own, weight in zip(refs[:count], refs[count:]):
        product = jnp.dot(own[...], weight[...], preferred_element_type=jnp.float32)
        total = product if total is None else total + product
    out_ref[...] = total


def late_kernel(_, sum_ref, residual_ref, *refs):
    *refs, out_ref = refs
    count = len(refs) // 3
    half = out_ref.shape[0] // 2
    for part in range(2):
        rows = slice(part * half, (part + 1) * half)
        total = sum_ref[rows, :] + residual_ref[rows, :].astype(jnp.float32)
        for own, weight in zip(refs[part * count : (part + 1) * count], refs[2 * count :]):
            total = total + jnp.dot(own[...], weight[...], preferred_element_type=jnp.float32)
        out_ref[rows, :] = total.astype(jnp.bfloat16)


TILE = 256


def project(kernel, name, heads, tiled, whole, weight, out_type):
    rows, features = tiled[0].shape if tiled else (whole[0].shape[0], weight.shape[1])
    depth = whole[0].shape[1]
    count = heads.shape[0]
    specs = [pl.BlockSpec((rows, TILE), lambda j, at: (0, j)) for _ in tiled]
    specs += [pl.BlockSpec(value.shape, lambda j, at: (0, 0)) for value in whole]
    specs += [pl.BlockSpec((depth, TILE), lambda j, at, i=i: (at[i], j)) for i in range(count)]
    return pl.pallas_call(
        kernel,
        grid_spec=pltpu.PrefetchScalarGridSpec(
            num_scalar_prefetch=1,
            grid=(features // TILE,),
            in_specs=specs,
            out_specs=pl.BlockSpec((rows, TILE), lambda j, at: (0, j)),
        ),
        out_shape=jax.ShapeDtypeStruct((rows, features), out_type),
        compiler_params=pltpu.CompilerParams(vmem_limit_bytes=40 << 20),
        cost_estimate=pl.CostEstimate(
            flops=2 * rows * features * depth * count, bytes_accessed=4 * rows * features, transcendentals=0
        ),
        name=name,
    )(heads, *tiled, *whole, *([weight] * count))


def swap(value):
    return lax.all_to_all(value, "seq", split_axis=0, concat_axis=0, tiled=True)


def shards(queries, residual, nbr_kv, nbr_owner, nbr_slot, out_weight):
    tok_rows, width = queries.shape
    blocks = tok_rows // BLOCK
    seq_count = lax.axis_size("seq")
    places = seq_count * NAMED
    all_weight = lax.all_gather(out_weight, "seq", axis=0, tiled=True)

    owners = nbr_owner.reshape(-1)
    position = jnp.arange(owners.shape[0], dtype=jnp.int32)
    earlier = (owners[:, None] == owners[None, :]) & (position[None, :] < position[:, None])
    target = owners * NAMED + jnp.sum(earlier.astype(jnp.int32), axis=1)
    place = jnp.arange(places, dtype=jnp.int32)
    match = (place[:, None] == target[None, :]).astype(jnp.int32)
    asked = jnp.sum(match * (nbr_slot.reshape(-1) + 1)[None, :], axis=1)

    first_next = lax.ppermute(queries[:BLOCK], "seq", [(s, s - 1) for s in range(1, seq_count)])
    chunks = queries.reshape(blocks, BLOCK, width)
    pack = like((seq_count, NAMED * BLOCK + STAT_ROWS, width))
    (sent,) = call(send_kernel, "send", [target, asked], [chunks, first_next], [pack], 16)
    arrived = swap(sent)
    heard = arrived[:, NAMED * BLOCK, :NAMED].astype(jnp.int32).reshape(-1)
    (partial,) = call(
        attend_kernel,
        "attend",
        [heard],
        [arrived, nbr_kv],
        [like((places, BLOCK + STAT_ROWS, width))],
        40,
        [pltpu.SMEM((places,), jnp.int32)],
    )
    moved, last = call(
        combine_kernel, "combine", [target], [swap(partial)], [like((blocks, BLOCK, width)), like((BLOCK, width))], 32
    )
    carried = lax.ppermute(last, "seq", [(s, s + 1) for s in range(seq_count - 1)])
    chunk = lax.broadcasted_iota(jnp.int32, (blocks, 1, 1), 0)
    row = lax.broadcasted_iota(jnp.int32, (1, BLOCK, 1), 1)
    placed = jnp.where((chunk == 0) & (row < KEPT), carried[None], moved).reshape(tok_rows, width)
    return project_rows(placed, all_weight, residual)


def project_rows(placed, all_weight, residual):
    head_count = lax.axis_size("head")
    chips = head_count // 2
    half = placed.shape[0] // 2
    me = lax.axis_index("head")
    chip, core = me // 2, me % 2

    def along(value, step):
        return lax.ppermute(value, "head", [(h, (h + 2 * step) % head_count) for h in range(head_count)])

    def across(value):
        return lax.ppermute(value, "head", [(h, h ^ 1) for h in range(head_count)])

    def name(step, other):
        return (chip + step) % chips * 2 + (core + other) % 2

    up, down = along(placed, 1), along(placed, -1)
    far_up, far_down = along(up[:half], 1), along(down[half:], -1)
    pieces = [placed, across(placed), up, across(up), down, across(down)]
    heads = jnp.stack([name(step, other) for step in (0, -1, 1) for other in (0, 1)])
    total = project(early_kernel, "early", heads, [], pieces, all_weight, jnp.float32)
    late = [far_up, across(far_up), far_down, across(far_down)]
    heads = jnp.stack([name(2, 0), name(2, 1)])
    return project(late_kernel, "late", heads, [total, residual], late, all_weight, jnp.bfloat16)


def solution(mesh):
    return jax.shard_map(
        shards,
        mesh=mesh,
        in_specs=(
            P("seq", "head"),
            P("seq", "head"),
            P("seq", None, None, "head"),
            P("seq", None),
            P("seq", None),
            P("seq", "head"),
        ),
        out_specs=P("seq", "head"),
        check_vma=False,
    )
```

```python
import functools

import jax
import jax.numpy as jnp
from jax import lax
from jax.experimental import pallas as pl
from jax.experimental.pallas import tpu as pltpu
from jax.sharding import PartitionSpec as P

HDIM = 128
BLOCK = 64
KEPT = BLOCK - 1
STAT_ROWS = 8
INFO_ROWS = 16
ROUND_Y = 4
ROUND_Z = 8
PAIR = 2 * HDIM
AT_ONCE = 4
TILE = 256
VMEM = pl.BlockSpec(memory_space=pltpu.VMEM)
SMEM = pl.BlockSpec(memory_space=pltpu.SMEM)


def call(kernel, name, scalars, inputs, outputs, limit, scratch=(), aliases=None, out_specs=None):
    return pl.pallas_call(
        kernel,
        grid_spec=pltpu.PrefetchScalarGridSpec(
            num_scalar_prefetch=len(scalars),
            grid=(),
            in_specs=[VMEM] * len(inputs),
            out_specs=out_specs or [VMEM] * len(outputs),
            scratch_shapes=scratch,
        ),
        out_shape=outputs,
        input_output_aliases=aliases or {},
        compiler_params=pltpu.CompilerParams(vmem_limit_bytes=limit << 20),
        name=name,
    )(*scalars, *inputs)


def like(shape, dtype=jnp.bfloat16):
    return jax.ShapeDtypeStruct(shape, dtype)


def turn_kernel(info_ref, query_ref, next_ref, out_ref):
    blocks, rows, width = query_ref.shape
    kept = lax.broadcasted_iota(jnp.int32, (rows, width), 0) < rows - 1
    for block in range(blocks):
        after = query_ref[block + 1] if block + 1 < blocks else next_ref[...]
        out_ref[block * rows : (block + 1) * rows, :] = jnp.where(kept, after, query_ref[block])
    out_ref[blocks * rows :, :] = info_ref[...]


def pack_stats(top, total):
    value = jnp.concatenate([top, total], axis=1)
    high = value.astype(jnp.bfloat16).astype(jnp.float32)
    rest = value - high
    middle = rest.astype(jnp.bfloat16).astype(jnp.float32)
    zero = jnp.zeros((STAT_ROWS - 3, PAIR), jnp.float32)
    return jnp.concatenate([high, middle, rest - middle, zero], axis=0).astype(jnp.bfloat16)


def read_stats(rows):
    rows = rows.astype(jnp.float32)
    value = rows[0:1] + rows[1:2] + rows[2:3]
    return value[:, :HDIM], value[:, HDIM:]


def merged(one, other, one_stats, other_stats):
    (top_a, sum_a), (top_b, sum_b) = read_stats(one_stats), read_stats(other_stats)
    live_a, live_b = sum_a > 0, sum_b > 0
    top_a, top_b = jnp.where(live_a, top_a, top_b), jnp.where(live_b, top_b, top_a)
    joint = jnp.maximum(top_a, top_b)
    factor_a = jnp.where(live_a, jnp.exp(top_a - joint) * sum_a, 0.0)
    factor_b = jnp.where(live_b, jnp.exp(top_b - joint) * sum_b, 0.0)
    whole = factor_a + factor_b
    shares = [factor_a / whole, factor_b / whole, jnp.zeros((STAT_ROWS - 2, HDIM), jnp.float32)]
    columns = jnp.concatenate(shares, axis=0).T
    values = []
    for head in range(2):
        own, cols = slice(head * BLOCK, (head + 1) * BLOCK), slice(head * HDIM, (head + 1) * HDIM)
        a, b = columns[own, 0:1], columns[own, 1:2]
        values.append(
            jnp.where(a > 0, a * one[:, cols].astype(jnp.float32), 0.0)
            + jnp.where(b > 0, b * other[:, cols].astype(jnp.float32), 0.0)
        )
    return jnp.concatenate(values, axis=1), joint, whole


def attend_kernel(first, meta, place, *refs):
    queries, refs = refs[:ROUND_Z], refs[ROUND_Z:]
    stores, (out_ref, starts, blocks, chosen, listed, counts, slots) = refs[:5], refs[5:]
    per = meta.shape[0] // (2 * ROUND_Z)
    for store in range(5):
        counts[store] = 0
    count = jnp.int32(0)
    for asker in range(ROUND_Z):
        starts[asker] = count

        def note(index, count, asker=asker):
            owner = meta[2 * per * asker + index]
            slot = meta[2 * per * asker + per + index]
            here = lax.rem(owner, ROUND_Z) == place[1]

            @pl.when(here)
            def _():
                away = lax.rem(lax.div(owner, ROUND_Z) - place[0] + ROUND_Y, ROUND_Y)
                late = (away == 2) & (slot >= 8)
                store = jnp.where(late, 4, away)
                block = lax.div(index, 2)
                blocks[count] = block
                slots[count] = jnp.where(late, slot - 8, slot)
                at = counts[store]
                listed[store * out_ref.shape[0] + at] = count
                counts[store] = at + 1
                start = pl.multiple_of(block * BLOCK, BLOCK)
                chosen[count] = queries[asker][pl.ds(start, BLOCK), first : first + PAIR]

            return count + here.astype(jnp.int32)

        count = lax.fori_loop(0, per, note, count)
    starts[ROUND_Z] = count
    zero = jnp.zeros((BLOCK, HDIM), jnp.bfloat16)

    for store, kv_ref in enumerate(stores):

        def some(index, carry, store=store, kv_ref=kv_ref):
            work = []
            for other in range(AT_ONCE):
                at = listed[store * out_ref.shape[0] + jnp.minimum(index * AT_ONCE + other, counts[store] - 1)]
                work.append((at, slots[at]))
            scores = []
            for at, slot in work:
                left, right = chosen[at, :, :HDIM], chosen[at, :, HDIM:]
                both = jnp.concatenate(
                    [jnp.concatenate([left, zero], axis=1), jnp.concatenate([zero, right], axis=1)], axis=0
                )
                scores.append(
                    lax.dot_general(
                        kv_ref[slot, 0], both, (((1,), (1,)), ((), ())), preferred_element_type=jnp.float32
                    )
                    * HDIM ** (-0.5)
                )
            tops = [jnp.max(score, axis=0, keepdims=True) for score in scores]
            weights = [jnp.exp(score - top) for score, top in zip(scores, tops)]
            totals = [jnp.sum(weight, axis=0, keepdims=True) for weight in weights]
            shares = [(weight * (1.0 / total)).astype(jnp.bfloat16) for weight, total in zip(weights, totals)]
            for (at, slot), share, top, total in zip(work, shares, tops, totals):
                blended = lax.dot_general(
                    share, kv_ref[slot, 1], (((0,), (0,)), ((), ())), preferred_element_type=jnp.float32
                )
                out_ref[at, :BLOCK, :HDIM] = blended[:BLOCK, :HDIM].astype(jnp.bfloat16)
                out_ref[at, :BLOCK, HDIM:] = blended[BLOCK:, HDIM:].astype(jnp.bfloat16)
                out_ref[at, BLOCK:, :] = pack_stats(top, total)
            return carry

        lax.fori_loop(0, lax.div(counts[store] + AT_ONCE - 1, AT_ONCE), some, 0)


def add_parts(asker, starts, blocks, parts_ref, out_ref):
    def one(index, carry):
        block = blocks[index]
        value, top, total = merged(
            out_ref[block, :BLOCK, :], parts_ref[index, :BLOCK, :], out_ref[block, BLOCK:, :], parts_ref[index, BLOCK:, :]
        )
        out_ref[block, :BLOCK, :] = value.astype(jnp.bfloat16)
        out_ref[block, BLOCK:, :] = pack_stats(top, total)
        return carry

    lax.fori_loop(starts[asker], starts[asker + 1], one, 0)


def begin_kernel(askers, starts, blocks, parts_ref, *outs):
    for asker, out_ref in zip(askers, outs):
        for block in range(out_ref.shape[0]):
            out_ref[block, BLOCK:, :] = jnp.zeros((STAT_ROWS, PAIR), jnp.bfloat16)
        add_parts(asker, starts, blocks, parts_ref, out_ref)


def hop_kernel(asker, starts, blocks, parts_ref, in_ref, out_ref):
    add_parts(asker, starts, blocks, parts_ref, out_ref)


def end_kernel(starts, blocks, own_ref, down_ref, up_ref, out_ref, last_ref):
    count = out_ref.shape[0]
    kept = lax.broadcasted_iota(jnp.int32, (BLOCK, PAIR), 0) < KEPT

    def joined(block):
        value, top, total = merged(
            down_ref[block, :BLOCK, :], up_ref[block, :BLOCK, :], down_ref[block, BLOCK:, :], up_ref[block, BLOCK:, :]
        )
        return value.astype(jnp.bfloat16)

    before = joined(0)
    out_ref[0] = before
    for block in range(1, count):
        now = joined(block)
        out_ref[block] = jnp.where(kept, before, now)
        before = now
    last_ref[...] = before


def project_kernel(tiles, full, far, _, *refs):
    *refs, out_ref = refs
    tiled, refs = refs[:tiles], refs[tiles:]
    whole, refs = refs[:full], refs[full:]
    halves, weights = refs[: 2 * far], refs[2 * far :]
    half = out_ref.shape[0] // 2
    for part in range(2):
        rows = slice(part * half, (part + 1) * half)
        total = None
        pieces = [ref[rows, :] for ref in whole] + [ref[...] for ref in halves[part * far : (part + 1) * far]]
        for ref in tiled:
            value = ref[rows, :].astype(jnp.float32)
            total = value if total is None else total + value
        for piece, weight in zip(pieces, weights):
            product = jnp.dot(piece, weight[...], preferred_element_type=jnp.float32)
            total = product if total is None else total + product
        out_ref[rows, :] = total.astype(out_ref.dtype)


def project(name, groups, tiled, whole, halves, weight, rows, out_type):
    features = weight.shape[1]
    far, count = len(halves) // 2, groups.shape[0]
    specs = [pl.BlockSpec((rows, TILE), lambda j, at: (0, j)) for _ in tiled]
    specs += [pl.BlockSpec(value.shape, lambda j, at: (0, 0)) for value in whole + halves]
    specs += [pl.BlockSpec((PAIR, TILE), lambda j, at, i=i: (at[i], j)) for i in range(count)]
    return pl.pallas_call(
        functools.partial(project_kernel, len(tiled), len(whole), far),
        grid_spec=pltpu.PrefetchScalarGridSpec(
            num_scalar_prefetch=1,
            grid=(features // TILE,),
            in_specs=specs,
            out_specs=pl.BlockSpec((rows, TILE), lambda j, at: (0, j)),
        ),
        out_shape=like((rows, features), out_type),
        compiler_params=pltpu.CompilerParams(vmem_limit_bytes=40 << 20),
        cost_estimate=pl.CostEstimate(
            flops=2 * rows * features * PAIR * count, bytes_accessed=4 * rows * features, transcendentals=0
        ),
        name=name,
    )(groups, *tiled, *whole, *halves, *([weight] * count))


def along_y(value, step):
    pairs = [(s, (s // ROUND_Z + step) % ROUND_Y * ROUND_Z + s % ROUND_Z) for s in range(ROUND_Y * ROUND_Z)]
    return lax.ppermute(value, "seq", pairs)


def along_z(value, step):
    pairs = [(s, s // ROUND_Z * ROUND_Z + (s + step) % ROUND_Z) for s in range(ROUND_Y * ROUND_Z)]
    return lax.ppermute(value, "seq", pairs)


def along_x(value, step):
    return lax.ppermute(value, "head", [(h, (h + 2 * step) % 8) for h in range(8)])


def across(value):
    return lax.ppermute(value, "head", [(h, h ^ 1) for h in range(8)])


def shards(queries, residual, nbr_kv, nbr_owner, nbr_slot, out_weight):
    tok_rows, width = queries.shape
    blocks = tok_rows // BLOCK
    seq_count = lax.axis_size("seq")
    me = lax.axis_index("seq")
    place = jnp.stack([me // ROUND_Z, me % ROUND_Z]).astype(jnp.int32)
    per = 2 * blocks
    all_weight = lax.all_gather(out_weight, "seq", axis=0, tiled=True)

    first_next = lax.ppermute(queries[:BLOCK], "seq", [(s, s - 1) for s in range(1, seq_count)])
    info = jnp.concatenate([nbr_owner.reshape(-1), nbr_slot.reshape(-1)]).astype(jnp.bfloat16)
    info = jnp.pad(info[None], ((0, INFO_ROWS - 1), (0, width - 2 * per)))
    chunks = queries.reshape(blocks, BLOCK, width)
    (own,) = call(turn_kernel, "turn", [], [info, chunks, first_next], [like((tok_rows + INFO_ROWS, width))], 16)
    down, up = [own], [own]
    for step in range(4):
        down.append(along_z(down[-1], 1))
        if step < 3:
            up.append(along_z(up[-1], -1))
    asked = down + up[1:]
    meta = jnp.concatenate([value[tok_rows, : 2 * per] for value in asked]).astype(jnp.int32)

    placed = []
    most = 8 * ROUND_Z
    for first in range(0, width, PAIR):
        here = nbr_kv[..., first : first + PAIR]
        before, after = along_y(here, 1), along_y(here, -1)
        low, high = along_y(before[:8], 1), along_y(after[8:], -1)
        parts, starts, places = call(
            functools.partial(attend_kernel, first),
            "attend",
            [meta, place],
            asked + [here, after, low, before, high],
            [like((most, BLOCK + STAT_ROWS, PAIR)), like((ROUND_Z + 1,), jnp.int32), like((most,), jnp.int32)],
            48,
            [
                pltpu.VMEM((most, BLOCK, PAIR), jnp.bfloat16),
                pltpu.SMEM((5 * most,), jnp.int32),
                pltpu.SMEM((5,), jnp.int32),
                pltpu.SMEM((most,), jnp.int32),
            ],
            out_specs=[VMEM, SMEM, SMEM],
        )
        chunk = like((blocks, BLOCK + STAT_ROWS, PAIR))
        lists = [starts, places]
        back, forth = call(functools.partial(begin_kernel, (4, 7)), "begin", lists, [parts], [chunk, chunk], 16)
        for asker in (3, 2, 1, 0):
            back = along_z(back, -1)
            (back,) = call(functools.partial(hop_kernel, asker), "hop", lists, [parts, back], [chunk], 16, aliases={3: 0})
        for asker in (6, 5):
            forth = along_z(forth, 1)
            (forth,) = call(functools.partial(hop_kernel, asker), "hop", lists, [parts, forth], [chunk], 16, aliases={3: 0})
        forth = along_z(forth, 1)
        moved, last = call(
            end_kernel, "end", lists, [parts, back, forth], [like((blocks, BLOCK, PAIR)), like((BLOCK, PAIR))], 16
        )
        carried = lax.ppermute(last, "seq", [(s, s + 1) for s in range(seq_count - 1)])
        chunk_at = lax.broadcasted_iota(jnp.int32, (blocks, 1, 1), 0)
        row = lax.broadcasted_iota(jnp.int32, (1, BLOCK, 1), 1)
        fixed = jnp.where((chunk_at == 0) & (row < KEPT), carried[None], moved)
        placed.append(fixed.reshape(tok_rows, PAIR))
    return project_rows(placed, all_weight, residual)


def project_rows(placed, all_weight, residual):
    me = lax.axis_index("head")
    rows = residual.shape[0]
    half = rows // 2

    def groups(steps, part):
        named = [(me // 2 + step) % 4 * 2 + (me + other) % 2 for step in steps for other in (0, 1)]
        return jnp.stack([2 * name + part for name in named]).astype(jnp.int32)

    total = None
    for part, value in enumerate(placed):
        up, down = along_x(value, 1), along_x(value, -1)
        far_up, far_down = along_x(up[:half], 1), along_x(down[half:], -1)
        near = [value, across(value), up, across(up), down, across(down)]
        far = [far_up, across(far_up), far_down, across(far_down)]
        if part == 0:
            total = project("project", groups((0, -1, 1, 2), 0), [], near, far, all_weight, rows, jnp.float32)
        else:
            total = project("early", groups((0, -1, 1), 1), [total], near, [], all_weight, rows, jnp.float32)
            total = project("late", groups((2,), 1), [total, residual], [], far, all_weight, rows, jnp.bfloat16)
    return total


def solution(mesh):
    return jax.shard_map(
        shards,
        mesh=mesh,
        in_specs=(
            P("seq", "head"),
            P("seq", "head"),
            P("seq", None, None, "head"),
            P("seq", None),
            P("seq", None),
            P("seq", "head"),
        ),
        out_specs=P("seq", "head"),
        check_vma=False,
    )
```

```python
import functools

import jax
import jax.numpy as jnp
from jax import lax
from jax.experimental import pallas as pl
from jax.experimental.pallas import tpu as pltpu
from jax.sharding import PartitionSpec as P

HDIM = 128
BLOCK = 64
KEPT = BLOCK - 1
STAT_ROWS = 8
INFO_ROWS = 16
ROUND_Y = 4
ROUND_Z = 8
PAIR = 2 * HDIM
STORES = 5
AT_ONCE = 4
TILE = 256
VMEM = pl.BlockSpec(memory_space=pltpu.VMEM)
SMEM = pl.BlockSpec(memory_space=pltpu.SMEM)


def call(kernel, name, scalars, inputs, outputs, limit, scratch=(), aliases=None, in_specs=None, out_specs=None):
    return pl.pallas_call(
        kernel,
        grid_spec=pltpu.PrefetchScalarGridSpec(
            num_scalar_prefetch=len(scalars),
            grid=(),
            in_specs=in_specs or [VMEM] * len(inputs),
            out_specs=out_specs or [VMEM] * len(outputs),
            scratch_shapes=scratch,
        ),
        out_shape=outputs,
        input_output_aliases=aliases or {},
        compiler_params=pltpu.CompilerParams(vmem_limit_bytes=limit << 20),
        name=name,
    )(*scalars, *inputs)


def like(shape, dtype=jnp.bfloat16):
    return jax.ShapeDtypeStruct(shape, dtype)


def turn_kernel(info_ref, query_ref, next_ref, out_ref):
    blocks, rows, width = query_ref.shape
    kept = lax.broadcasted_iota(jnp.int32, (rows, width), 0) < rows - 1
    for block in range(blocks):
        after = query_ref[block + 1] if block + 1 < blocks else next_ref[...]
        out_ref[block * rows : (block + 1) * rows, :] = jnp.where(kept, after, query_ref[block])
    out_ref[blocks * rows :, :] = info_ref[...]


def pack_stats(top, total):
    value = jnp.concatenate([top, total], axis=1)
    high = value.astype(jnp.bfloat16).astype(jnp.float32)
    rest = value - high
    middle = rest.astype(jnp.bfloat16).astype(jnp.float32)
    zero = jnp.zeros((STAT_ROWS - 3, PAIR), jnp.float32)
    return jnp.concatenate([high, middle, rest - middle, zero], axis=0).astype(jnp.bfloat16)


def read_stats(rows):
    rows = rows.astype(jnp.float32)
    value = rows[0:1] + rows[1:2] + rows[2:3]
    return value[:, :HDIM], value[:, HDIM:]


def merged(one, other, one_stats, other_stats):
    (top_a, sum_a), (top_b, sum_b) = read_stats(one_stats), read_stats(other_stats)
    live_a, live_b = sum_a > 0, sum_b > 0
    top_a, top_b = jnp.where(live_a, top_a, top_b), jnp.where(live_b, top_b, top_a)
    joint = jnp.maximum(top_a, top_b)
    factor_a = jnp.where(live_a, jnp.exp(top_a - joint) * sum_a, 0.0)
    factor_b = jnp.where(live_b, jnp.exp(top_b - joint) * sum_b, 0.0)
    whole = factor_a + factor_b
    shares = [factor_a / whole, factor_b / whole, jnp.zeros((STAT_ROWS - 2, HDIM), jnp.float32)]
    columns = jnp.concatenate(shares, axis=0).T
    values = []
    for head in range(2):
        own, cols = slice(head * BLOCK, (head + 1) * BLOCK), slice(head * HDIM, (head + 1) * HDIM)
        a, b = columns[own, 0:1], columns[own, 1:2]
        values.append(
            jnp.where(a > 0, a * one[:, cols].astype(jnp.float32), 0.0)
            + jnp.where(b > 0, b * other[:, cols].astype(jnp.float32), 0.0)
        )
    return jnp.concatenate(values, axis=1), joint, whole


def plan_kernel(meta, place, *refs):
    queries, (*picked, starts, blocks, slots, listed, counts) = refs[:ROUND_Z], refs[ROUND_Z:]
    most = blocks.shape[0]
    per = meta.shape[0] // (2 * ROUND_Z)
    for store in range(STORES):
        counts[store] = 0
    count = jnp.int32(0)
    for asker in range(ROUND_Z):
        starts[asker] = count

        def note(index, count, asker=asker):
            owner = meta[2 * per * asker + index]
            slot = meta[2 * per * asker + per + index]
            here = lax.rem(owner, ROUND_Z) == place[1]

            @pl.when(here)
            def _():
                away = lax.rem(lax.div(owner, ROUND_Z) - place[0] + ROUND_Y, ROUND_Y)
                late = (away == 2) & (slot >= 8)
                store = jnp.where(late, 4, away)
                block = lax.div(index, 2)
                blocks[count] = block
                slots[count] = jnp.where(late, slot - 8, slot)
                at = counts[store]
                listed[store * most + at] = count
                counts[store] = at + 1
                start = pl.multiple_of(block * BLOCK, BLOCK)
                for part, ref in enumerate(picked):
                    ref[count] = queries[asker][pl.ds(start, BLOCK), part * PAIR : (part + 1) * PAIR]

            return count + here.astype(jnp.int32)

        count = lax.fori_loop(0, per, note, count)
    starts[ROUND_Z] = count


def attend_kernel(slots, listed, counts, chosen, *refs):
    stores, (out_ref, *held, arrived) = refs[:STORES], refs[STORES:]
    most = out_ref.shape[0]
    copies = [pltpu.make_async_copy(ref, own, arrived.at[i]) for i, (ref, own) in enumerate(zip(stores, held))]
    for copy in copies:
        copy.start()
    zero = jnp.zeros((BLOCK, HDIM), jnp.bfloat16)

    for store, kv_ref in enumerate(held):
        copies[store].wait()

        def some(index, carry, store=store, kv_ref=kv_ref):
            work = []
            for other in range(AT_ONCE):
                at = listed[store * most + jnp.minimum(index * AT_ONCE + other, counts[store] - 1)]
                work.append((at, slots[at]))
            scores = []
            for at, slot in work:
                left, right = chosen[at, :, :HDIM], chosen[at, :, HDIM:]
                both = jnp.concatenate(
                    [jnp.concatenate([left, zero], axis=1), jnp.concatenate([zero, right], axis=1)], axis=0
                )
                scores.append(
                    lax.dot_general(
                        kv_ref[slot, 0], both, (((1,), (1,)), ((), ())), preferred_element_type=jnp.float32
                    )
                    * HDIM ** (-0.5)
                )
            tops = [jnp.max(score, axis=0, keepdims=True) for score in scores]
            weights = [jnp.exp(score - top) for score, top in zip(scores, tops)]
            totals = [jnp.sum(weight, axis=0, keepdims=True) for weight in weights]
            shares = [(weight * (1.0 / total)).astype(jnp.bfloat16) for weight, total in zip(weights, totals)]
            for (at, slot), share, top, total in zip(work, shares, tops, totals):
                blended = lax.dot_general(
                    share, kv_ref[slot, 1], (((0,), (0,)), ((), ())), preferred_element_type=jnp.float32
                )
                out_ref[at, :BLOCK, :HDIM] = blended[:BLOCK, :HDIM].astype(jnp.bfloat16)
                out_ref[at, :BLOCK, HDIM:] = blended[BLOCK:, HDIM:].astype(jnp.bfloat16)
                out_ref[at, BLOCK:, :] = pack_stats(top, total)
            return carry

        lax.fori_loop(0, lax.div(counts[store] + AT_ONCE - 1, AT_ONCE), some, 0)


def add_parts(asker, starts, blocks, parts_ref, out_ref):
    def one(index, carry):
        block = blocks[index]
        value, top, total = merged(
            out_ref[block, :BLOCK, :], parts_ref[index, :BLOCK, :], out_ref[block, BLOCK:, :], parts_ref[index, BLOCK:, :]
        )
        out_ref[block, :BLOCK, :] = value.astype(jnp.bfloat16)
        out_ref[block, BLOCK:, :] = pack_stats(top, total)
        return carry

    lax.fori_loop(starts[asker], starts[asker + 1], one, 0)


def begin_kernel(askers, starts, blocks, parts_ref, *outs):
    for asker, out_ref in zip(askers, outs):
        for block in range(out_ref.shape[0]):
            out_ref[block, BLOCK:, :] = jnp.zeros((STAT_ROWS, PAIR), jnp.bfloat16)
        add_parts(asker, starts, blocks, parts_ref, out_ref)


def hop_kernel(asker, starts, blocks, parts_ref, in_ref, out_ref):
    add_parts(asker, starts, blocks, parts_ref, out_ref)


def end_kernel(down_ref, up_ref, out_ref, last_ref):
    count = out_ref.shape[0]
    kept = lax.broadcasted_iota(jnp.int32, (BLOCK, PAIR), 0) < KEPT

    def joined(block):
        value, top, total = merged(
            down_ref[block, :BLOCK, :], up_ref[block, :BLOCK, :], down_ref[block, BLOCK:, :], up_ref[block, BLOCK:, :]
        )
        return value.astype(jnp.bfloat16)

    before = joined(0)
    out_ref[0] = before
    for block in range(1, count):
        now = joined(block)
        out_ref[block] = jnp.where(kept, before, now)
        before = now
    last_ref[...] = before


def project_kernel(tiles, full, far, _, *refs):
    *refs, out_ref = refs
    tiled, refs = refs[:tiles], refs[tiles:]
    whole, refs = refs[:full], refs[full:]
    halves, weights = refs[: 2 * far], refs[2 * far :]
    half = out_ref.shape[0] // 2
    for part in range(2):
        rows = slice(part * half, (part + 1) * half)
        total = None
        pieces = [ref[rows, :] for ref in whole] + [ref[...] for ref in halves[part * far : (part + 1) * far]]
        for ref in tiled:
            value = ref[rows, :].astype(jnp.float32)
            total = value if total is None else total + value
        for piece, top, bottom in zip(pieces, weights[0::2], weights[1::2]):
            weight = jnp.concatenate([top[0, 0], bottom[0, 0]], axis=0)
            product = jnp.dot(piece, weight, preferred_element_type=jnp.float32)
            total = product if total is None else total + product
        out_ref[rows, :] = total.astype(out_ref.dtype)


def project(name, groups, tiled, whole, halves, weight, rows, out_type):
    features = weight.shape[3]
    far, count = len(halves) // 2, groups.shape[0] // 2
    specs = [pl.BlockSpec((rows, TILE), lambda j, at: (0, j)) for _ in tiled]
    specs += [pl.BlockSpec(value.shape, lambda j, at: (0, 0)) for value in whole + halves]
    specs += [pl.BlockSpec((1, 1, HDIM, TILE), lambda j, at, i=i: (at[2 * i], at[2 * i + 1], 0, j)) for i in range(count)]
    return pl.pallas_call(
        functools.partial(project_kernel, len(tiled), len(whole), far),
        grid_spec=pltpu.PrefetchScalarGridSpec(
            num_scalar_prefetch=1,
            grid=(features // TILE,),
            in_specs=specs,
            out_specs=pl.BlockSpec((rows, TILE), lambda j, at: (0, j)),
        ),
        out_shape=like((rows, features), out_type),
        compiler_params=pltpu.CompilerParams(vmem_limit_bytes=24 << 20),
        cost_estimate=pl.CostEstimate(
            flops=2 * rows * features * HDIM * count, bytes_accessed=4 * rows * features, transcendentals=0
        ),
        name=name,
    )(groups, *tiled, *whole, *halves, *([weight] * count))


def after(value, *others):
    corners = [other[(slice(0, 1),) * other.ndim] for other in others]
    return lax.optimization_barrier((value, *corners))[0]


def along_y(value, step):
    pairs = [(s, (s // ROUND_Z + step) % ROUND_Y * ROUND_Z + s % ROUND_Z) for s in range(ROUND_Y * ROUND_Z)]
    return lax.ppermute(value, "seq", pairs)


def along_z(value, step):
    pairs = [(s, s // ROUND_Z * ROUND_Z + (s + step) % ROUND_Z) for s in range(ROUND_Y * ROUND_Z)]
    return lax.ppermute(value, "seq", pairs)


def along_x(value, step):
    return lax.ppermute(value, "head", [(h, (h + 2 * step) % 8) for h in range(8)])


def across(value):
    return lax.ppermute(value, "head", [(h, h ^ 1) for h in range(8)])


def shards(queries, residual, nbr_kv, nbr_owner, nbr_slot, out_weight):
    tok_rows, width = queries.shape
    blocks = tok_rows // BLOCK
    seq_count = lax.axis_size("seq")
    me = lax.axis_index("seq")
    place = jnp.stack([me // ROUND_Z, me % ROUND_Z]).astype(jnp.int32)
    per = 2 * blocks
    first_next = lax.ppermute(queries[:BLOCK], "seq", [(s, s - 1) for s in range(1, seq_count)])
    info = jnp.concatenate([nbr_owner.reshape(-1), nbr_slot.reshape(-1)]).astype(jnp.bfloat16)
    info = jnp.pad(info[None], ((0, INFO_ROWS - 1), (0, width - 2 * per)))
    chunks = queries.reshape(blocks, BLOCK, width)
    (own,) = call(turn_kernel, "turn", [], [info, chunks, first_next], [like((tok_rows + INFO_ROWS, width))], 16)
    down, up = [own], [own]
    for step in range(4):
        down.append(along_z(down[-1], 1))
        if step < 3:
            up.append(along_z(up[-1], -1))
    asked = down + up[1:]
    meta = jnp.concatenate([value[tok_rows, : 2 * per] for value in asked]).astype(jnp.int32)

    all_weight = lax.all_gather(out_weight, "seq", axis=0).reshape((ROUND_Y, ROUND_Z) + out_weight.shape)

    most = 8 * ROUND_Z
    numbers = [like((size,), jnp.int32) for size in (ROUND_Z + 1, most, most, STORES * most, STORES)]
    parts_count = width // PAIR
    *picked, starts, places, slots, listed, counts = call(
        plan_kernel,
        "plan",
        [meta, place],
        asked,
        [like((most, BLOCK, PAIR))] * parts_count + numbers,
        32,
        out_specs=[VMEM] * parts_count + [SMEM] * len(numbers),
    )
    placed = []
    done = []
    for part in range(parts_count):
        here = nbr_kv[..., part * PAIR : (part + 1) * PAIR]
        if done:
            here = after(here, *done)
        before, behind = along_y(here, 1), along_y(here, -1)
        low, high = along_y(before[:8], 1), along_y(behind[8:], -1)
        done = [low, high]
        stores = [here, behind, low, before, high]
        (parts,) = call(
            attend_kernel,
            "attend",
            [slots, listed, counts],
            [picked[part]] + stores,
            [like((most, BLOCK + STAT_ROWS, PAIR))],
            24,
            [pltpu.VMEM(value.shape, value.dtype) for value in stores] + [pltpu.SemaphoreType.DMA((STORES,))],
            in_specs=[VMEM] + [pl.BlockSpec(memory_space=pl.ANY)] * STORES,
        )
        chunk = like((blocks, BLOCK + STAT_ROWS, PAIR))
        lists = [starts, places]
        back, forth = call(functools.partial(begin_kernel, (4, 7)), "begin", lists, [parts], [chunk, chunk], 16)
        for asker in (3, 2, 1, 0):
            back = along_z(back, -1)
            (back,) = call(functools.partial(hop_kernel, asker), "hop", lists, [parts, back], [chunk], 16, aliases={3: 0})
        for asker in (6, 5):
            forth = along_z(forth, 1)
            (forth,) = call(functools.partial(hop_kernel, asker), "hop", lists, [parts, forth], [chunk], 16, aliases={3: 0})
        forth = along_z(forth, 1)
        moved, last = call(
            end_kernel, "end", [], [back, forth], [like((blocks, BLOCK, PAIR)), like((BLOCK, PAIR))], 16
        )
        carried = lax.ppermute(last, "seq", [(s, s + 1) for s in range(seq_count - 1)])
        chunk_at = lax.broadcasted_iota(jnp.int32, (blocks, 1, 1), 0)
        row = lax.broadcasted_iota(jnp.int32, (1, BLOCK, 1), 1)
        fixed = jnp.where((chunk_at == 0) & (row < KEPT), carried[None], moved)
        placed.append(fixed.reshape(tok_rows, PAIR))
    return project_rows(placed, all_weight, residual)


def project_rows(placed, all_weight, residual):
    me = lax.axis_index("head")
    rows = residual.shape[0]
    half = rows // 2

    def groups(steps, part):
        named = [((me // 2 + step) % 4, (me + other) % 2) for step in steps for other in (0, 1)]
        spots = [(chip, 4 * core + 2 * part + h) for chip, core in named for h in (0, 1)]
        return jnp.stack([n for spot in spots for n in spot]).astype(jnp.int32)

    total = None
    for part, value in enumerate(placed):
        up, down = along_x(value, 1), along_x(value, -1)
        far_up, far_down = along_x(up[:half], 1), along_x(down[half:], -1)
        near = [value, across(value), up, across(up), down, across(down)]
        far = [far_up, across(far_up), far_down, across(far_down)]
        if part == 0:
            total = project("project", groups((0, -1, 1, 2), 0), [], near, far, all_weight, rows, jnp.float32)
        else:
            total = project("early", groups((0, -1, 1), 1), [total], near, [], all_weight, rows, jnp.float32)
            total = project("late", groups((2,), 1), [total, residual], [], far, all_weight, rows, jnp.bfloat16)
    return total


def solution(mesh):
    return jax.shard_map(
        shards,
        mesh=mesh,
        in_specs=(
            P("seq", "head"),
            P("seq", "head"),
            P("seq", None, None, "head"),
            P("seq", None),
            P("seq", None),
            P("seq", "head"),
        ),
        out_specs=P("seq", "head"),
        check_vma=False,
    )
```

```python
import functools

import jax
import jax.numpy as jnp
from jax import lax
from jax.experimental import pallas as pl
from jax.experimental.pallas import tpu as pltpu
from jax.sharding import PartitionSpec as P

HDIM = 128
BLOCK = 64
KEPT = BLOCK - 1
STAT_ROWS = 8
INFO_ROWS = 16
ROUND_Y = 4
ROUND_Z = 8
PAIR = 2 * HDIM
STORES = 5
AT_ONCE = 4
TILE = 256
VMEM = pl.BlockSpec(memory_space=pltpu.VMEM)
SMEM = pl.BlockSpec(memory_space=pltpu.SMEM)


def call(kernel, name, scalars, inputs, outputs, limit, scratch=(), aliases=None, in_specs=None, out_specs=None):
    return pl.pallas_call(
        kernel,
        grid_spec=pltpu.PrefetchScalarGridSpec(
            num_scalar_prefetch=len(scalars),
            grid=(),
            in_specs=in_specs or [VMEM] * len(inputs),
            out_specs=out_specs or [VMEM] * len(outputs),
            scratch_shapes=scratch,
        ),
        out_shape=outputs,
        input_output_aliases=aliases or {},
        compiler_params=pltpu.CompilerParams(vmem_limit_bytes=limit << 20),
        name=name,
    )(*scalars, *inputs)


def like(shape, dtype=jnp.bfloat16):
    return jax.ShapeDtypeStruct(shape, dtype)


def turn_kernel(info_ref, query_ref, next_ref, out_ref):
    blocks, rows, width = query_ref.shape
    kept = lax.broadcasted_iota(jnp.int32, (rows, width), 0) < rows - 1
    for block in range(blocks):
        after = query_ref[block + 1] if block + 1 < blocks else next_ref[...]
        out_ref[block * rows : (block + 1) * rows, :] = jnp.where(kept, after, query_ref[block])
    out_ref[blocks * rows :, :] = info_ref[...]


def pack_stats(top, total):
    value = jnp.concatenate([top, total], axis=1)
    high = value.astype(jnp.bfloat16).astype(jnp.float32)
    rest = value - high
    middle = rest.astype(jnp.bfloat16).astype(jnp.float32)
    zero = jnp.zeros((STAT_ROWS - 3, PAIR), jnp.float32)
    return jnp.concatenate([high, middle, rest - middle, zero], axis=0).astype(jnp.bfloat16)


def read_stats(rows):
    rows = rows.astype(jnp.float32)
    value = rows[0:1] + rows[1:2] + rows[2:3]
    return value[:, :HDIM], value[:, HDIM:]


def merged(one, other, one_stats, other_stats):
    (top_a, sum_a), (top_b, sum_b) = read_stats(one_stats), read_stats(other_stats)
    live_a, live_b = sum_a > 0, sum_b > 0
    top_a, top_b = jnp.where(live_a, top_a, top_b), jnp.where(live_b, top_b, top_a)
    joint = jnp.maximum(top_a, top_b)
    factor_a = jnp.where(live_a, jnp.exp(top_a - joint) * sum_a, 0.0)
    factor_b = jnp.where(live_b, jnp.exp(top_b - joint) * sum_b, 0.0)
    whole = factor_a + factor_b
    shares = [factor_a / whole, factor_b / whole, jnp.zeros((STAT_ROWS - 2, HDIM), jnp.float32)]
    columns = jnp.concatenate(shares, axis=0).T
    values = []
    for head in range(2):
        own, cols = slice(head * BLOCK, (head + 1) * BLOCK), slice(head * HDIM, (head + 1) * HDIM)
        a, b = columns[own, 0:1], columns[own, 1:2]
        values.append(
            jnp.where(a > 0, a * one[:, cols].astype(jnp.float32), 0.0)
            + jnp.where(b > 0, b * other[:, cols].astype(jnp.float32), 0.0)
        )
    return jnp.concatenate(values, axis=1), joint, whole


def plan_kernel(meta, place, *refs):
    queries, (*picked, starts, blocks, slots, listed, counts) = refs[:ROUND_Z], refs[ROUND_Z:]
    most = blocks.shape[0]
    per = meta.shape[0] // (2 * ROUND_Z)
    for store in range(STORES):
        counts[store] = 0
    count = jnp.int32(0)
    for asker in range(ROUND_Z):
        starts[asker] = count

        def note(index, count, asker=asker):
            owner = meta[2 * per * asker + index]
            slot = meta[2 * per * asker + per + index]
            here = lax.rem(owner, ROUND_Z) == place[1]

            @pl.when(here)
            def _():
                away = lax.rem(lax.div(owner, ROUND_Z) - place[0] + ROUND_Y, ROUND_Y)
                late = (away == 2) & (slot >= 8)
                store = jnp.where(late, 4, away)
                block = lax.div(index, 2)
                blocks[count] = block
                slots[count] = jnp.where(late, slot - 8, slot)
                at = counts[store]
                listed[store * most + at] = count
                counts[store] = at + 1
                start = pl.multiple_of(block * BLOCK, BLOCK)
                for part, ref in enumerate(picked):
                    ref[count] = queries[asker][pl.ds(start, BLOCK), part * PAIR : (part + 1) * PAIR]

            return count + here.astype(jnp.int32)

        count = lax.fori_loop(0, per, note, count)
    starts[ROUND_Z] = count


def attend_kernel(slots, listed, counts, chosen, *refs):
    stores, (out_ref, *held, arrived) = refs[:STORES], refs[STORES:]
    most = out_ref.shape[0]
    copies = [pltpu.make_async_copy(ref, own, arrived.at[i]) for i, (ref, own) in enumerate(zip(stores, held))]
    for copy in copies:
        copy.start()
    zero = jnp.zeros((BLOCK, HDIM), jnp.bfloat16)

    for store, kv_ref in enumerate(held):
        copies[store].wait()

        def some(index, carry, store=store, kv_ref=kv_ref):
            work = []
            for other in range(AT_ONCE):
                at = listed[store * most + jnp.minimum(index * AT_ONCE + other, counts[store] - 1)]
                work.append((at, slots[at]))
            scores = []
            for at, slot in work:
                left, right = chosen[at, :, :HDIM], chosen[at, :, HDIM:]
                both = jnp.concatenate(
                    [jnp.concatenate([left, zero], axis=1), jnp.concatenate([zero, right], axis=1)], axis=0
                )
                scores.append(
                    lax.dot_general(
                        kv_ref[slot, 0], both, (((1,), (1,)), ((), ())), preferred_element_type=jnp.float32
                    )
                    * HDIM ** (-0.5)
                )
            tops = [jnp.max(score, axis=0, keepdims=True) for score in scores]
            weights = [jnp.exp(score - top) for score, top in zip(scores, tops)]
            totals = [jnp.sum(weight, axis=0, keepdims=True) for weight in weights]
            shares = [(weight * (1.0 / total)).astype(jnp.bfloat16) for weight, total in zip(weights, totals)]
            for (at, slot), share, top, total in zip(work, shares, tops, totals):
                blended = lax.dot_general(
                    share, kv_ref[slot, 1], (((0,), (0,)), ((), ())), preferred_element_type=jnp.float32
                )
                out_ref[at, :BLOCK, :HDIM] = blended[:BLOCK, :HDIM].astype(jnp.bfloat16)
                out_ref[at, :BLOCK, HDIM:] = blended[BLOCK:, HDIM:].astype(jnp.bfloat16)
                out_ref[at, BLOCK:, :] = pack_stats(top, total)
            return carry

        lax.fori_loop(0, lax.div(counts[store] + AT_ONCE - 1, AT_ONCE), some, 0)


def add_parts(asker, starts, blocks, parts_ref, out_ref):
    def one(index, carry):
        block = blocks[index]
        value, top, total = merged(
            out_ref[block, :BLOCK, :], parts_ref[index, :BLOCK, :], out_ref[block, BLOCK:, :], parts_ref[index, BLOCK:, :]
        )
        out_ref[block, :BLOCK, :] = value.astype(jnp.bfloat16)
        out_ref[block, BLOCK:, :] = pack_stats(top, total)
        return carry

    lax.fori_loop(starts[asker], starts[asker + 1], one, 0)


def begin_kernel(askers, starts, blocks, parts_ref, *outs):
    for asker, out_ref in zip(askers, outs):
        for block in range(out_ref.shape[0]):
            out_ref[block, BLOCK:, :] = jnp.zeros((STAT_ROWS, PAIR), jnp.bfloat16)
        add_parts(asker, starts, blocks, parts_ref, out_ref)


def hop_kernel(asker, starts, blocks, parts_ref, in_ref, out_ref):
    add_parts(asker, starts, blocks, parts_ref, out_ref)


def end_kernel(down_ref, up_ref, out_ref, last_ref):
    count = out_ref.shape[0]
    kept = lax.broadcasted_iota(jnp.int32, (BLOCK, PAIR), 0) < KEPT

    def joined(block):
        value, top, total = merged(
            down_ref[block, :BLOCK, :], up_ref[block, :BLOCK, :], down_ref[block, BLOCK:, :], up_ref[block, BLOCK:, :]
        )
        return value.astype(jnp.bfloat16)

    before = joined(0)
    out_ref[0] = before
    for block in range(1, count):
        now = joined(block)
        out_ref[block] = jnp.where(kept, before, now)
        before = now
    last_ref[...] = before


def project_kernel(tiles, full, far, _, *refs):
    *refs, out_ref = refs
    tiled, refs = refs[:tiles], refs[tiles:]
    whole, refs = refs[:full], refs[full:]
    halves, weights = refs[: 2 * far], refs[2 * far :]
    half = out_ref.shape[0] // 2
    for part in range(2):
        rows = slice(part * half, (part + 1) * half)
        total = None
        pieces = [ref[rows, :] for ref in whole] + [ref[...] for ref in halves[part * far : (part + 1) * far]]
        for ref in tiled:
            value = ref[rows, :].astype(jnp.float32)
            total = value if total is None else total + value
        for piece, top, bottom in zip(pieces, weights[0::2], weights[1::2]):
            weight = jnp.concatenate([top[0, 0], bottom[0, 0]], axis=0)
            product = jnp.dot(piece, weight, preferred_element_type=jnp.float32)
            total = product if total is None else total + product
        out_ref[rows, :] = total.astype(out_ref.dtype)


def project(name, groups, tiled, whole, halves, weight, rows, out_type):
    features = weight.shape[3]
    far, count = len(halves) // 2, groups.shape[0] // 2
    specs = [pl.BlockSpec((rows, TILE), lambda j, at: (0, j)) for _ in tiled]
    specs += [pl.BlockSpec(value.shape, lambda j, at: (0, 0)) for value in whole + halves]
    specs += [pl.BlockSpec((1, 1, HDIM, TILE), lambda j, at, i=i: (at[2 * i], at[2 * i + 1], 0, j)) for i in range(count)]
    return pl.pallas_call(
        functools.partial(project_kernel, len(tiled), len(whole), far),
        grid_spec=pltpu.PrefetchScalarGridSpec(
            num_scalar_prefetch=1,
            grid=(features // TILE,),
            in_specs=specs,
            out_specs=pl.BlockSpec((rows, TILE), lambda j, at: (0, j)),
        ),
        out_shape=like((rows, features), out_type),
        compiler_params=pltpu.CompilerParams(vmem_limit_bytes=24 << 20),
        cost_estimate=pl.CostEstimate(
            flops=2 * rows * features * HDIM * count, bytes_accessed=4 * rows * features, transcendentals=0
        ),
        name=name,
    )(groups, *tiled, *whole, *halves, *([weight] * count))


def after(value, *others):
    corners = [other[(0,) * other.ndim].astype(jnp.float32) for other in others]
    never = functools.reduce(jnp.logical_or, [jnp.abs(corner) > 1e30 for corner in corners])
    return jnp.where(never, jnp.zeros_like(value), value)


def along_y(value, step):
    pairs = [(s, (s // ROUND_Z + step) % ROUND_Y * ROUND_Z + s % ROUND_Z) for s in range(ROUND_Y * ROUND_Z)]
    return lax.ppermute(value, "seq", pairs)


def along_z(value, step):
    pairs = [(s, s // ROUND_Z * ROUND_Z + (s + step) % ROUND_Z) for s in range(ROUND_Y * ROUND_Z)]
    return lax.ppermute(value, "seq", pairs)


def along_x(value, step):
    return lax.ppermute(value, "head", [(h, (h + 2 * step) % 8) for h in range(8)])


def across(value):
    return lax.ppermute(value, "head", [(h, h ^ 1) for h in range(8)])


def shards(queries, residual, nbr_kv, nbr_owner, nbr_slot, out_weight):
    tok_rows, width = queries.shape
    blocks = tok_rows // BLOCK
    seq_count = lax.axis_size("seq")
    me = lax.axis_index("seq")
    place = jnp.stack([me // ROUND_Z, me % ROUND_Z]).astype(jnp.int32)
    per = 2 * blocks
    first_next = lax.ppermute(queries[:BLOCK], "seq", [(s, s - 1) for s in range(1, seq_count)])
    info = jnp.concatenate([nbr_owner.reshape(-1), nbr_slot.reshape(-1)]).astype(jnp.bfloat16)
    info = jnp.pad(info[None], ((0, INFO_ROWS - 1), (0, width - 2 * per)))
    chunks = queries.reshape(blocks, BLOCK, width)
    (own,) = call(turn_kernel, "turn", [], [info, chunks, first_next], [like((tok_rows + INFO_ROWS, width))], 16)
    down, up = [own], [own]
    for step in range(4):
        down.append(along_z(down[-1], 1))
        if step < 3:
            up.append(along_z(up[-1], -1))
    asked = down + up[1:]
    meta = jnp.concatenate([value[tok_rows, : 2 * per] for value in asked]).astype(jnp.int32)

    all_weight = lax.all_gather(out_weight, "seq", axis=0).reshape((ROUND_Y, ROUND_Z) + out_weight.shape)

    most = 8 * ROUND_Z
    numbers = [like((size,), jnp.int32) for size in (ROUND_Z + 1, most, most, STORES * most, STORES)]
    parts_count = width // PAIR
    *picked, starts, places, slots, listed, counts = call(
        plan_kernel,
        "plan",
        [meta, place],
        asked,
        [like((most, BLOCK, PAIR))] * parts_count + numbers,
        32,
        out_specs=[VMEM] * parts_count + [SMEM] * len(numbers),
    )
    placed = []
    done = []
    for part in range(parts_count):
        here = nbr_kv[..., part * PAIR : (part + 1) * PAIR]
        if done:
            here = after(here, *done, down[-1], up[-1])
            slots = after(slots, last)
        before, behind = along_y(here, 1), along_y(here, -1)
        low, high = along_y(before[:8], 1), along_y(behind[8:], -1)
        done = [low, high]
        stores = [here, behind, low, before, high]
        (parts,) = call(
            attend_kernel,
            "attend",
            [slots, listed, counts],
            [picked[part]] + stores,
            [like((most, BLOCK + STAT_ROWS, PAIR))],
            24,
            [pltpu.VMEM(value.shape, value.dtype) for value in stores] + [pltpu.SemaphoreType.DMA((STORES,))],
            in_specs=[VMEM] + [pl.BlockSpec(memory_space=pl.ANY)] * STORES,
        )
        chunk = like((blocks, BLOCK + STAT_ROWS, PAIR))
        lists = [starts, places]
        back, forth = call(functools.partial(begin_kernel, (4, 7)), "begin", lists, [parts], [chunk, chunk], 16)
        for asker in (3, 2, 1, 0):
            back = along_z(back, -1)
            (back,) = call(functools.partial(hop_kernel, asker), "hop", lists, [parts, back], [chunk], 16, aliases={3: 0})
        for asker in (6, 5):
            forth = along_z(forth, 1)
            (forth,) = call(functools.partial(hop_kernel, asker), "hop", lists, [parts, forth], [chunk], 16, aliases={3: 0})
        forth = along_z(forth, 1)
        moved, last = call(
            end_kernel, "end", [], [back, forth], [like((blocks, BLOCK, PAIR)), like((BLOCK, PAIR))], 16
        )
        carried = lax.ppermute(last, "seq", [(s, s + 1) for s in range(seq_count - 1)])
        chunk_at = lax.broadcasted_iota(jnp.int32, (blocks, 1, 1), 0)
        row = lax.broadcasted_iota(jnp.int32, (1, BLOCK, 1), 1)
        fixed = jnp.where((chunk_at == 0) & (row < KEPT), carried[None], moved)
        placed.append(fixed.reshape(tok_rows, PAIR))
    return project_rows(placed, all_weight, residual)


def project_rows(placed, all_weight, residual):
    me = lax.axis_index("head")
    rows = residual.shape[0]
    half = rows // 2

    def groups(steps, part):
        named = [((me // 2 + step) % 4, (me + other) % 2) for step in steps for other in (0, 1)]
        spots = [(chip, 4 * core + 2 * part + h) for chip, core in named for h in (0, 1)]
        return jnp.stack([n for spot in spots for n in spot]).astype(jnp.int32)

    total = None
    for part, value in enumerate(placed):
        up, down = along_x(value, 1), along_x(value, -1)
        far_up, far_down = along_x(up[:half], 1), along_x(down[half:], -1)
        near = [value, across(value), up, across(up), down, across(down)]
        far = [far_up, across(far_up), far_down, across(far_down)]
        if part == 0:
            total = project("project", groups((0, -1, 1, 2), 0), [], near, far, all_weight, rows, jnp.float32)
        else:
            total = project("early", groups((0, -1, 1), 1), [total], near, [], all_weight, rows, jnp.float32)
            total = project("late", groups((2,), 1), [total, residual], [], far, all_weight, rows, jnp.bfloat16)
    return total


def solution(mesh):
    return jax.shard_map(
        shards,
        mesh=mesh,
        in_specs=(
            P("seq", "head"),
            P("seq", "head"),
            P("seq", None, None, "head"),
            P("seq", None),
            P("seq", None),
            P("seq", "head"),
        ),
        out_specs=P("seq", "head"),
        check_vma=False,
    )
```
